1024 devices in a mesh: expert: 32 (over z_lo, core), fsdp: 4 (over x), dp: 8 (over z_hi, y).
Axes of the slice: x: 4, y: 4, z: 32 (z_hi: 2, z_lo: 16; z = z_hi * 16 + z_lo), core: 2. Of those that a mesh axis runs over, the one named last changes fastest.
Arguments:
- tokens: bfloat16 [131072, 1664], P(('expert', 'fsdp', 'dp')), may hold values from -6 to 6
- grad_out: bfloat16 [131072, 1664], P(('expert', 'fsdp', 'dp')), may hold values from -0.29882812 to 0.29882812
- slot_token: int32 [1024, 32, 2], P(('expert', 'fsdp', 'dp')), may hold values from 0 to 127
- slot_gate: float32 [1024, 32, 2], P(('expert', 'fsdp', 'dp')), may hold values from 0.1 to 1
- w_in: bfloat16 [32, 4096, 1664], P('expert', 'fsdp'), may hold values from -0.15625 to 0.15625
- w_out: bfloat16 [32, 4096, 1664], P('expert', 'fsdp'), may hold values from -0.09375 to 0.09375
Outputs:
- mixed: bfloat16 [131072, 1664], P(('expert', 'fsdp', 'dp'))
- weight_grad: float32 [32, 4096, 1664], P('expert', ('fsdp', 'dp'))
The draws below stay inside these ranges and needn't reach their ends.
Inputs may be any that keep to these rules, and one draw needn't show every extreme that they name: `slot_token`: each slot names a token of its own shard; a token may fill several slots or none.
All inputs are finite; a program needn't handle non-finite values.
Results may differ from the reference program's by a relative error of at most 0.017.
Values may be sent and summed in bfloat16 or wider, within the bound.
A program may use at most 64 MiB of HBM per device.

```python
import jax
import jax.numpy as jnp
from jax import lax

D = 1664
HID = 4096
EXPERTS = 32
TOK_DEV = 128
CAP = 2
SHARDS = 1024
REPLICAS = 8
TOKENS = 131072


def set_ends(result, own_key, smallest, high):
    dims = result.shape
    spot = [jax.random.randint(jax.random.fold_in(own_key, axis), (), 0, dims[axis]) for axis in range(len(dims))]
    result = result.at[tuple(spot)].set(smallest)
    longest = dims.index(max(dims))
    spot[longest] = (spot[longest] + 1) % dims[longest]
    return result.at[tuple(spot)].set(high)


def levels(stream_key, shape, shards, least, high):
    gain = 1.0
    for position, parts in shards:
        heights = jax.random.uniform(jax.random.fold_in(jax.random.fold_in(stream_key, 6), position), (parts,), jnp.float32, least / len(shards), high / len(shards))
        gain = gain * jnp.repeat(jnp.exp(heights), shape[position] // parts).reshape((-1,) + (1,) * (len(shape) - 1 - position))
    return gain


def gaussian(rng, shape, width, limit, cuts=(), held_as=jnp.bfloat16):
    gain = levels(rng, shape, cuts, -0.22, 0.18) if cuts else 1.0
    entries = jax.random.normal(rng, shape, jnp.float32) * width * gain
    return jnp.minimum(jnp.maximum(entries, -limit), limit).astype(held_as)


def setup_inputs(seed: int = 0) -> dict:
    key_of = jax.random.split(jax.random.key(seed), 7)
    return {
        "tokens": gaussian(key_of[0], (TOKENS, D), 1.0, 6.0, ((0, 1024),)),
        "grad_out": gaussian(key_of[1], (TOKENS, D), 0.05, 0.29882812, ((0, 1024),)),
        "slot_token": set_ends(jax.random.randint(key_of[2], (SHARDS, EXPERTS, CAP), 0, TOK_DEV), jax.random.fold_in(key_of[2], 1), 0, TOK_DEV - 1).astype(jnp.int32),
        "slot_gate": jnp.clip(0.1 + 0.9 * jax.random.uniform(key_of[3], (SHARDS, EXPERTS, CAP), jnp.float32) ** levels(key_of[3], (SHARDS, EXPERTS, CAP), ((0, 1024),), -0.2, 0.2), 0.1, 1.0),
        "w_in": gaussian(key_of[4], (EXPERTS, HID, D), D ** -0.5, 0.15625, ((0, 32), (1, 4))),
        "w_out": gaussian(key_of[5], (EXPERTS, HID, D), HID ** -0.5, 0.09375, ((0, 32), (1, 4))),
    }


def gelu_parts(value):
    normal_cdf = 0.5 * (1.0 + jax.scipy.special.erf(value * 0.7071067811865476))
    normal_pdf = jnp.exp(-0.5 * value * value) * 0.3989422804014327
    return value * normal_cdf, normal_cdf + value * normal_pdf


def reference(tokens, grad_out, slot_token, slot_gate, w_in, w_out):
    shard_tok = tokens.reshape(SHARDS, TOK_DEV, D)
    shard_grad = grad_out.reshape(SHARDS, TOK_DEV, D)
    flat_index = slot_token.reshape(SHARDS, EXPERTS * CAP)
    picked_in = jax.vmap(lambda table, where: table[where])(shard_tok, flat_index)
    picked_grad = jax.vmap(lambda table, where: table[where])(shard_grad, flat_index)
    gate_col = slot_gate.reshape(SHARDS, EXPERTS * CAP, 1)
    slot_grad = (gate_col * picked_grad.astype(jnp.float32)).astype(jnp.bfloat16)
    by_expert_in = picked_in.reshape(SHARDS, EXPERTS, CAP, D).transpose(1, 0, 2, 3)
    by_expert_grad = slot_grad.reshape(SHARDS, EXPERTS, CAP, D).transpose(1, 0, 2, 3)

    def one_expert(operands):
        x_slots, g_slots, weight_in, weight_out = operands
        x_rows = x_slots.reshape(SHARDS * CAP, D)
        g_rows = g_slots.reshape(SHARDS * CAP, D)
        pre = lax.dot_general(x_rows, weight_in, (((1,), (1,)), ((), ())), preferred_element_type=jnp.float32)
        act_value, slope = gelu_parts(pre)
        act = act_value.astype(jnp.bfloat16)
        expert_out = jnp.dot(act, weight_out, preferred_element_type=jnp.float32).astype(jnp.bfloat16)
        back = lax.dot_general(g_rows, weight_out, (((1,), (1,)), ((), ())), preferred_element_type=jnp.float32)
        dpre = (back * slope).astype(jnp.bfloat16)
        x_four = x_rows.reshape(SHARDS // REPLICAS, REPLICAS, CAP, D).astype(jnp.float32)
        d_four = dpre.reshape(SHARDS // REPLICAS, REPLICAS, CAP, HID).astype(jnp.float32)
        partial_value = jnp.einsum('grch,grcd->rhd', d_four, x_four).astype(jnp.bfloat16)
        partial_value = lax.optimization_barrier(partial_value)
        grad = jnp.sum(partial_value.astype(jnp.float32), axis=0)
        return expert_out.reshape(SHARDS, CAP, D), grad

    outputs, weight_grad = lax.map(one_expert, (by_expert_in, by_expert_grad, w_in, w_out))
    outputs = outputs.transpose(1, 0, 2, 3).astype(jnp.float32)
    chosen = (slot_token[..., None] == jnp.arange(TOK_DEV, dtype=jnp.int32)).astype(jnp.float32)
    combine = chosen * slot_gate[..., None]
    mixed = jnp.einsum('sect,secd->std', combine, outputs, precision=lax.Precision.HIGHEST)
    return mixed.reshape(TOKENS, D).astype(jnp.bfloat16), weight_grad
```

```python
import functools

import jax
import jax.numpy as jnp
from jax import lax
from jax.experimental import pallas as pl
from jax.experimental.pallas import tpu as pltpu
from jax.sharding import PartitionSpec as P

MESH = pl.DeviceIdType.MESH
BF16 = jnp.bfloat16
F32 = jnp.float32
NT = (((1,), (1,)), ((), ()))


def gelu_parts(value):
    normal_cdf = 0.5 * (1.0 + lax.erf(value * 0.7071067811865476))
    normal_pdf = jnp.exp(-0.5 * value * value) * 0.3989422804014327
    return (value * normal_cdf, normal_cdf + value * normal_pdf)


def column_pieces(width):
    unit = 128
    total = width // unit
    if total < 5:
        return [(i * unit, unit) for i in range(total)]
    sizes = [2]
    rest = total - 2
    parts = 3
    for i in range(parts):
        sizes.append(rest // parts + (1 if i < rest % parts else 0))
    pieces, start = [], 0
    for size in sizes:
        pieces.append((start * unit, size * unit))
        start += size
    return pieces


def layer_kernel(
    dims, idx_col, gate_col, idx_row, gate_row, tokens, grad_out, w_in, w_out,
    mixed, weight_grad,
    win, wout, snd, xg, xs, gs, act, slope, dpre_t, po, po_in, own_po, back_rows, ret,
    gsend, gin, gown, zsend, zin,
    w_sem, z_send, z_recv, x_send, x_recv, po_send, po_recv, r_send, r_recv,
    y_send, y_recv, zz_send, zz_recv,
):
    zl_n, x_n, y_n = dims
    z_n = 2 * zl_n
    half = zl_n // 2
    rounds = zl_n - 1
    experts = 2 * zl_n
    width = tokens.shape[1]
    toks = tokens.shape[0]
    hid = w_in.shape[0]
    slots = 2 * experts
    rows = x_n * slots
    block = hid // (2 * y_n)
    e_me = lax.axis_index("expert")
    x_me = lax.axis_index("fsdp")
    d_me = lax.axis_index("dp")
    core = e_me % 2
    zh = d_me // y_n
    y_me = d_me % y_n
    z_me = zh * zl_n + e_me // 2

    def at_z(z, c):
        return ((z % zl_n) * 2 + c, x_me, (z // zl_n) * y_n + y_me)

    def at_x(step):
        return (e_me, (x_me + step) % x_n, d_me)

    def at_y(step):
        return (e_me, x_me, zh * y_n + (y_me + step) % y_n)

    def distance(t, c):
        return (t // 2 + 1) * (1 - 2 * (t % 2)) - z_n // 2 * c * (t // (rounds - 1))

    mate = at_z(z_me, 1 - core)
    across = at_z((z_me + zl_n) % z_n, core)

    win_copy = pltpu.make_async_copy(w_in, win, w_sem.at[0])
    wout_copy = pltpu.make_async_copy(w_out, wout, w_sem.at[1])
    win_copy.start()
    wout_copy.start()

    barrier = pltpu.get_barrier_semaphore()

    def greet(device):
        pl.semaphore_signal(barrier, inc=1, device_id=device, device_id_type=MESH)

    def greet_z(i, carry):
        t = i // 2
        c = i % 2
        dz = (t // 2 + 1) * (1 - 2 * (t % 2))
        greet(at_z((z_me + dz + z_n) % z_n, c))
        return carry

    lax.fori_loop(0, 2 * (rounds - 1), greet_z, 0)
    greet(at_z((z_me + half) % z_n, 0))
    greet(at_z((z_me - half + z_n) % z_n, 1))
    greet(at_z((z_me - half + zl_n * core + z_n) % z_n, core))
    greet(mate)
    greet(across)
    for j in range(1, x_n):
        greet(at_x(j))
    for j in range(1, y_n):
        greet(at_y(j))

    lane = lax.broadcasted_iota(jnp.int32, (2 * slots, 2 * toks), 1)
    pick = (idx_col[...] == lane).astype(F32).astype(BF16)
    both = jnp.concatenate([tokens[...], grad_out[...]], axis=0)
    picked = jnp.dot(pick, both, preferred_element_type=F32) * gate_col[...]
    snd[...] = picked.astype(BF16).reshape(experts, 4, width)

    pl.semaphore_wait(barrier, 2 * (rounds - 1) + 3 + 2 + (x_n - 1) + (y_n - 1))

    def z_copy(i):
        t = i // 2
        c = i % 2
        z_to = (z_me + distance(t, c) + z_n) % z_n
        return pltpu.make_async_remote_copy(
            src_ref=snd.at[(z_to % zl_n) * 2 + c],
            dst_ref=xg.at[0, 2 + 2 * t + core],
            send_sem=z_send.at[2 + i],
            recv_sem=z_recv.at[2 + 2 * t + core],
            device_id=at_z(z_to, c),
            device_id_type=MESH,
        )

    def z_start(i, carry):
        z_copy(i).start()
        return carry

    lax.fori_loop(0, 2 * rounds, z_start, 0)
    mate_copy = pltpu.make_async_remote_copy(
        src_ref=snd.at[e_me + 1 - 2 * core],
        dst_ref=xg.at[0, core],
        send_sem=z_send.at[0],
        recv_sem=z_recv.at[core],
        device_id=mate,
        device_id_type=MESH,
    )
    mate_copy.start()
    xg[0, pl.ds(core, 1)] = snd[pl.ds(e_me, 1)]

    def z_arrived(k):
        pltpu.make_async_remote_copy(
            src_ref=snd.at[0], dst_ref=xg.at[0, k], send_sem=z_send.at[0],
            recv_sem=z_recv.at[k], device_id=mate, device_id_type=MESH,
        ).wait_recv()

    groups = 4
    per = experts // groups

    def x_copy(g, j):
        return pltpu.make_async_remote_copy(
            src_ref=xg.at[0, pl.ds(per * g, per)],
            dst_ref=xg.at[j, pl.ds(per * g, per)],
            send_sem=x_send.at[g, j],
            recv_sem=x_recv.at[g, j],
            device_id=at_x(j),
            device_id_type=MESH,
        )

    for g in range(groups):
        first = 2 if g == 0 else per * g
        if g == 0:
            z_arrived(1 - core)

        def wait_one(k, carry):
            z_arrived(k)
            return carry

        lax.fori_loop(first, per * (g + 1), wait_one, 0)
        for j in range(1, x_n):
            x_copy(g, j).start()
    for g in range(groups):
        for j in range(1, x_n):
            x_copy(g, j).wait_recv()

    everything = xg[...].reshape(x_n * experts, 4, width)
    xs[...] = everything[:, 0:2].reshape(rows, width)
    gs[...] = everything[:, 2:4].reshape(rows, width)

    win_copy.wait()
    wout_copy.wait()
    hb = min(256, hid)

    def project(b, carry):
        at = pl.ds(pl.multiple_of(b * hb, hb), hb)
        pre = lax.dot_general(xs[...], win[at], NT, preferred_element_type=F32)
        value, tilt = gelu_parts(pre)
        act[:, at] = value.astype(BF16)
        slope[:, at] = tilt
        return carry

    lax.fori_loop(0, hid // hb, project, 0)
    for start in range(0, width, 256):
        cols = slice(start, min(start + 256, width))
        part = jnp.dot(act[...], wout[:, cols], preferred_element_type=F32)
        own_po[:, cols] = part[0:slots]
        po[:, :, :, cols] = part[slots:rows].astype(BF16).reshape(x_n - 1, experts, 2, cols.stop - cols.start)

    def po_copy(j):
        return pltpu.make_async_remote_copy(
            src_ref=po.at[j - 1],
            dst_ref=po_in.at[j - 1],
            send_sem=po_send.at[j - 1],
            recv_sem=po_recv.at[j - 1],
            device_id=at_x(x_n - j),
            device_id_type=MESH,
        )

    for j in range(1, x_n):
        po_copy(j).start()

    def cotangent(b, carry):
        at = pl.ds(pl.multiple_of(b * hb, hb), hb)
        back = lax.dot_general(gs[...], wout[at], NT, preferred_element_type=F32)
        dpre_t[at] = (back * slope[:, at]).T.astype(BF16)
        return carry

    lax.fori_loop(0, hid // hb, cotangent, 0)

    pieces = column_pieces(width)
    quarter = y_n * block

    def y_copy(side, p, j):
        cols = pl.ds(*pieces[p])
        return pltpu.make_async_remote_copy(
            src_ref=gsend.at[side, (y_me + j) % y_n, :, cols],
            dst_ref=gin.at[side, j - 1, :, cols],
            send_sem=y_send.at[side, p, j - 1],
            recv_sem=y_recv.at[side, p, j - 1],
            device_id=at_y(j),
            device_id_type=MESH,
        )

    def gradients(side):
        where = (zh + 1 - side) % 2
        mine = dpre_t[pl.ds(pl.multiple_of(where * quarter, quarter), quarter)]
        for p, (start, size) in enumerate(pieces):
            for at in range(start, start + size, 256):
                cols = slice(at, min(at + 256, start + size))
                term = jnp.dot(mine, xs[:, cols], preferred_element_type=F32)
                gsend[side, :, :, cols] = term.astype(BF16).reshape(y_n, block, cols.stop - cols.start)
            for j in range(1, y_n):
                y_copy(side, p, j).start()

    def summed(side, p):
        start, size = pieces[p]
        cols = slice(start, start + size)
        for j in range(1, y_n):
            y_copy(side, p, j).wait_recv()
        total = gsend[side, pl.ds(y_me, 1), :, cols][0].astype(F32)
        for j in range(1, y_n):
            total = total + gin[side, j - 1, :, cols].astype(F32)
        return total

    def zz_copy(p):
        cols = pl.ds(*pieces[p])
        return pltpu.make_async_remote_copy(
            src_ref=zsend.at[:, cols],
            dst_ref=zin.at[:, cols],
            send_sem=zz_send.at[p],
            recv_sem=zz_recv.at[p],
            device_id=across,
            device_id_type=MESH,
        )

    def cross(p):
        start, size = pieces[p]
        zsend[:, start:start + size] = summed(0, p).astype(BF16)
        zz_copy(p).start()

    gradients(0)
    cross(0)

    for j in range(1, x_n):
        po_copy(j).wait_recv()
    out = own_po[...]
    for j in range(1, x_n):
        out = out + po_in[j - 1].reshape(slots, width).astype(F32)
    back_rows[...] = out.astype(BF16).reshape(experts, 2, width)

    def ret_copy(i):
        t = i // 2
        c = i % 2
        z_to = (z_me - distance(t, core) + z_n) % z_n
        return pltpu.make_async_remote_copy(
            src_ref=back_rows.at[2 + i],
            dst_ref=ret.at[e_me],
            send_sem=r_send.at[2 + i],
            recv_sem=r_recv.at[e_me],
            device_id=at_z(z_to, c),
            device_id_type=MESH,
        )

    def ret_start(i, carry):
        ret_copy(i).start()
        return carry

    lax.fori_loop(0, 2 * rounds, ret_start, 0)
    mate_back = pltpu.make_async_remote_copy(
        src_ref=back_rows.at[1 - core],
        dst_ref=ret.at[e_me],
        send_sem=r_send.at[0],
        recv_sem=r_recv.at[e_me],
        device_id=mate,
        device_id_type=MESH,
    )
    mate_back.start()
    ret[pl.ds(e_me, 1)] = back_rows[pl.ds(core, 1)]

    for p in range(1, len(pieces)):
        cross(p)
    gradients(1)

    def ret_arrived(e):
        pltpu.make_async_remote_copy(
            src_ref=back_rows.at[0], dst_ref=ret.at[e], send_sem=r_send.at[0],
            recv_sem=r_recv.at[e], device_id=mate, device_id_type=MESH,
        ).wait_recv()

    def ret_wait(i, carry):
        c = i % 2
        z_from = (z_me + distance(i // 2, c) + z_n) % z_n
        ret_arrived((z_from % zl_n) * 2 + c)
        return carry

    lax.fori_loop(0, 2 * rounds, ret_wait, 0)
    ret_arrived(e_me + 1 - 2 * core)
    token = lax.broadcasted_iota(jnp.int32, (toks, slots), 0)
    weight = jnp.where(token == idx_row[...], gate_row[...], 0.0)
    high = weight.astype(BF16)
    rest = weight - high.astype(F32)
    middle = rest.astype(BF16)
    low = (rest - middle.astype(F32)).astype(BF16)
    came = ret[...].reshape(slots, width)
    total = jnp.dot(low, came, preferred_element_type=F32)
    total = total + jnp.dot(middle, came, preferred_element_type=F32)
    total = total + jnp.dot(high, came, preferred_element_type=F32)
    mixed[...] = total.astype(BF16)

    for p, (start, size) in enumerate(pieces):
        near = summed(1, p)
        zz_copy(p).wait_recv()
        cols = slice(start, start + size)
        weight_grad[:, cols] = near + zin[:, cols].astype(F32)

    def z_sent(i, carry):
        z_copy(i).wait_send()
        ret_copy(i).wait_send()
        return carry

    lax.fori_loop(0, 2 * rounds, z_sent, 0)
    mate_copy.wait_send()
    mate_back.wait_send()
    for g in range(groups):
        for j in range(1, x_n):
            x_copy(g, j).wait_send()
    for j in range(1, x_n):
        po_copy(j).wait_send()
    for p in range(len(pieces)):
        for side in range(2):
            for j in range(1, y_n):
                y_copy(side, p, j).wait_send()
        zz_copy(p).wait_send()


def body(zl_n, y_n, x_n, tokens, grad_out, slot_token, slot_gate, w_in, w_out):
    experts = 2 * zl_n
    toks, width = tokens.shape
    hid = w_in.shape[1]
    slots = 2 * experts
    rows = x_n * slots
    block = hid // (2 * y_n)
    place = slot_token.reshape(experts, 2)
    gate = slot_gate.reshape(experts, 2)
    idx_col = jnp.concatenate([place, place + toks], axis=1).reshape(2 * slots, 1)
    gate_col = jnp.concatenate([jnp.ones_like(gate), gate], axis=1).reshape(2 * slots, 1)
    pieces = len(column_pieces(width))
    vmem = pl.BlockSpec(memory_space=pltpu.VMEM)
    hbm = pl.BlockSpec(memory_space=pl.ANY)
    dma = pltpu.SemaphoreType.DMA
    mixed, weight_grad = pl.pallas_call(
        functools.partial(layer_kernel, (zl_n, x_n, y_n)),
        out_shape=(
            jax.ShapeDtypeStruct((toks, width), BF16),
            jax.ShapeDtypeStruct((block, width), F32),
        ),
        in_specs=[vmem] * 6 + [hbm] * 2,
        out_specs=(vmem, vmem),
        scratch_shapes=[
            pltpu.VMEM((hid, width), BF16),
            pltpu.VMEM((hid, width), BF16),
            pltpu.VMEM((experts, 4, width), BF16),
            pltpu.VMEM((x_n, experts, 4, width), BF16),
            pltpu.VMEM((rows, width), BF16),
            pltpu.VMEM((rows, width), BF16),
            pltpu.VMEM((rows, hid), BF16),
            pltpu.VMEM((rows, hid), F32),
            pltpu.VMEM((hid, rows), BF16),
            pltpu.VMEM((x_n - 1, experts, 2, width), BF16),
            pltpu.VMEM((x_n - 1, experts, 2, width), BF16),
            pltpu.VMEM((slots, width), F32),
            pltpu.VMEM((experts, 2, width), BF16),
            pltpu.VMEM((experts, 2, width), BF16),
            pltpu.VMEM((2, y_n, block, width), BF16),
            pltpu.VMEM((2, y_n - 1, block, width), BF16),
            pltpu.VMEM((8, 128), F32),
            pltpu.VMEM((block, width), BF16),
            pltpu.VMEM((block, width), BF16),
            dma((2,)),
            dma((experts,)),
            dma((experts,)),
            dma((4, x_n)),
            dma((4, x_n)),
            dma((x_n,)),
            dma((x_n,)),
            dma((experts,)),
            dma((experts,)),
            dma((2, pieces, y_n)),
            dma((2, pieces, y_n)),
            dma((pieces,)),
            dma((pieces,)),
        ],
        compiler_params=pltpu.CompilerParams(
            collective_id=0, has_side_effects=True, vmem_limit_bytes=56 * 1024 * 1024
        ),
    )(
        idx_col, gate_col, slot_token.reshape(1, slots), slot_gate.reshape(1, slots),
        tokens, grad_out, w_in[0], w_out[0],
    )
    return mixed, weight_grad[None]


def solution(mesh):
    placed = (
        P(("expert", "fsdp", "dp"), None),
        P(("expert", "fsdp", "dp"), None),
        P(("expert", "fsdp", "dp"), None, None),
        P(("expert", "fsdp", "dp"), None, None),
        P("expert", "fsdp", None),
        P("expert", "fsdp", None),
    )
    sizes = (mesh.shape["expert"] // 2, mesh.shape["dp"] // 2, mesh.shape["fsdp"])
    return jax.shard_map(
        functools.partial(body, *sizes),
        mesh=mesh,
        in_specs=placed,
        out_specs=(P(("expert", "fsdp", "dp"), None), P("expert", ("fsdp", "dp"), None)),
        check_vma=False,
    )
```

```python
import functools

import jax
import jax.numpy as jnp
from jax import lax
from jax.experimental import pallas as pl
from jax.experimental.pallas import tpu as pltpu
from jax.sharding import PartitionSpec as P

MESH = pl.DeviceIdType.MESH
BF16 = jnp.bfloat16
F32 = jnp.float32
NT = (((1,), (1,)), ((), ()))


def gelu_parts(value):
    normal_cdf = 0.5 * (1.0 + lax.erf(value * 0.7071067811865476))
    normal_pdf = jnp.exp(-0.5 * value * value) * 0.3989422804014327
    return (value * normal_cdf, normal_cdf + value * normal_pdf)


def column_pieces(width):
    unit = 128
    units = width // unit
    sizes, left = [], units
    for size in (1, 2, 3, 3):
        if left > size:
            sizes.append(size)
            left -= size
    sizes.append(left)
    pieces, start = [], 0
    for size in sizes:
        pieces.append((start * unit, size * unit))
        start += size
    return pieces


def arrival_groups(experts):
    edges = [0]
    for tail in (22, 14, 6, 2, 0):
        if experts - tail > edges[-1]:
            edges.append(experts - tail)
    return list(zip(edges[:-1], edges[1:]))


def layer_kernel(
    dims, place, gate, tokens, grad_out, w_in, w_out,
    mixed, weight_grad,
    win, wout, snd, xg, xs, gs, act, dpre_t, po, po_in, own_po, back_rows, ret,
    gsend, gin, zsend, zin,
    w_sem, z_send, z_recv, x_send, x_recv, po_send, po_recv, r_send, r_recv,
    y_send, y_recv, zz_send, zz_recv,
):
    zl_n, x_n, y_n = dims
    z_n = 2 * zl_n
    half = zl_n // 2
    experts = 2 * zl_n
    width = tokens.shape[1]
    toks = tokens.shape[0]
    hid = w_in.shape[0]
    slots = 2 * experts
    rows = x_n * slots
    block = hid // (2 * y_n)
    e_me = lax.axis_index("expert")
    x_me = lax.axis_index("fsdp")
    d_me = lax.axis_index("dp")
    core = lax.rem(e_me, 2)
    zh = lax.div(d_me, y_n)
    y_me = lax.rem(d_me, y_n)
    z_me = zh * zl_n + lax.div(e_me, 2)

    def wrap(z):
        return lax.rem(z + z_n, z_n)

    def expert_at(z, c):
        return lax.rem(z, zl_n) * 2 + c

    def at_z(z, c):
        return (expert_at(z, c), x_me, lax.div(z, zl_n) * y_n + y_me)

    def at_x(step):
        return (e_me, lax.rem(x_me + step, x_n), d_me)

    def at_y(step):
        return (e_me, x_me, zh * y_n + lax.rem(y_me + step, y_n))

    mate = at_z(z_me, 1 - core)
    across = at_z(wrap(z_me + zl_n), core)

    win_copy = pltpu.make_async_copy(w_in, win, w_sem.at[0])
    wout_copy = pltpu.make_async_copy(w_out, wout, w_sem.at[1])
    win_copy.start()
    wout_copy.start()

    barrier = pltpu.get_barrier_semaphore()

    def greet(device):
        pl.semaphore_signal(barrier, inc=1, device_id=device, device_id_type=MESH)

    def greet_z(m, carry):
        for z in (wrap(z_me + m), wrap(z_me - m)):
            for c in (0, 1):
                greet(at_z(z, c))
        return carry

    lax.fori_loop(1, half, greet_z, 0)
    greet(at_z(wrap(z_me + half), 0))
    greet(at_z(wrap(z_me - half), 1))
    greet(at_z(wrap(z_me - half + zl_n * core), core))
    greet(mate)
    greet(across)
    for j in range(1, x_n):
        greet(at_x(j))
    for j in range(1, y_n):
        greet(at_y(j))

    def column(table, rows, per):
        row = lax.broadcasted_iota(jnp.int32, (rows, experts), 0)
        lane = lax.broadcasted_iota(jnp.int32, (rows, experts), 1)
        value = jnp.where((row & 1) == 0, table[0:1].astype(F32), table[1:2].astype(F32))
        mine = lax.shift_right_logical(row, per) == lane
        return jnp.sum(jnp.where(mine, value, 0.0), axis=1, keepdims=True)

    row = lax.broadcasted_iota(jnp.int32, (2 * slots, 1), 0)
    is_grad = (row & 2) == 2
    wanted = column(place[...], 2 * slots, 2) + jnp.where(is_grad, float(toks), 0.0)
    scale = jnp.where(is_grad, column(gate[...], 2 * slots, 2), 1.0)
    lane = lax.broadcasted_iota(jnp.int32, (2 * slots, 2 * toks), 1).astype(F32)
    pick = (wanted == lane).astype(F32).astype(BF16)
    both = jnp.concatenate([tokens[...], grad_out[...]], axis=0)
    picked = jnp.dot(pick, both, preferred_element_type=F32) * scale
    snd[...] = picked.astype(BF16).reshape(experts, 4, width)

    pl.semaphore_wait(barrier, 4 * (half - 1) + 3 + 2 + (x_n - 1) + (y_n - 1))

    def z_copy(z_to, c, slot):
        return pltpu.make_async_remote_copy(
            src_ref=snd.at[expert_at(z_to, c)],
            dst_ref=xg.at[0, slot + core],
            send_sem=z_send.at[slot + c],
            recv_sem=z_recv.at[slot + core],
            device_id=at_z(z_to, c),
            device_id_type=MESH,
        )

    mate_copy = pltpu.make_async_remote_copy(
        src_ref=snd.at[e_me + 1 - 2 * core],
        dst_ref=xg.at[0, core],
        send_sem=z_send.at[0],
        recv_sem=z_recv.at[core],
        device_id=mate,
        device_id_type=MESH,
    )
    mate_copy.start()
    xg[0, pl.ds(core, 1)] = snd[pl.ds(e_me, 1)]

    for c in (0, 1):

        def z_start(m, carry):
            slot = 4 * m - 2
            z_copy(wrap(z_me + m), c, slot).start()
            z_copy(wrap(z_me - m), c, slot + 2).start()
            return carry

        lax.fori_loop(1, half, z_start, 0)
        z_copy(wrap(z_me + half - zl_n * c), c, experts - 2).start()
    def z_arrived(k):
        pltpu.make_async_remote_copy(
            src_ref=snd.at[0], dst_ref=xg.at[0, k], send_sem=z_send.at[0],
            recv_sem=z_recv.at[k], device_id=mate, device_id_type=MESH,
        ).wait_recv()

    groups = arrival_groups(experts)

    def x_copy(g, j):
        first, last = groups[g]
        return pltpu.make_async_remote_copy(
            src_ref=xg.at[0, pl.ds(first, last - first)],
            dst_ref=xg.at[j, pl.ds(first, last - first)],
            send_sem=x_send.at[g, j],
            recv_sem=x_recv.at[g, j],
            device_id=at_x(j),
            device_id_type=MESH,
        )

    def wait_one(k, carry):
        z_arrived(k)
        return carry

    z_arrived(1 - core)
    for g, (first, last) in enumerate(groups):
        lax.fori_loop(max(first, 2), last, wait_one, 0)
        for j in range(1, x_n):
            x_copy(g, j).start()
    for g in range(len(groups)):
        for j in range(1, x_n):
            x_copy(g, j).wait_recv()

    everything = xg[...].reshape(x_n * experts, 4, width)
    xs[...] = everything[:, 0:2].reshape(rows, width)
    gs[...] = everything[:, 2:4].reshape(rows, width)

    win_copy.wait()
    wout_copy.wait()
    quarter = y_n * block
    hb = min(256, quarter)

    def hidden(side):
        def one(b, carry):
            at = pl.ds(pl.multiple_of(lax.rem(zh + 1 - side, 2) * quarter + b * hb, hb), hb)
            pre = lax.dot_general(xs[...], win[at], NT, preferred_element_type=F32)
            value, slope = gelu_parts(pre)
            act[:, at] = value.astype(BF16)
            back = lax.dot_general(gs[...], wout[at], NT, preferred_element_type=F32)
            dpre_t[at] = (back * slope).T.astype(BF16)
            return carry

        lax.fori_loop(0, quarter // hb, one, 0)

    def project_out():
        for start in range(0, width, 256):
            cols = slice(start, min(start + 256, width))
            part = jnp.dot(act[...], wout[:, cols], preferred_element_type=F32)
            own_po[:, cols] = part[0:slots]
            po[:, :, :, cols] = part[slots:rows].astype(BF16).reshape(x_n - 1, experts, 2, cols.stop - cols.start)
        for j in range(1, x_n):
            po_copy(j).start()

    def po_copy(j):
        return pltpu.make_async_remote_copy(
            src_ref=po.at[j - 1],
            dst_ref=po_in.at[j - 1],
            send_sem=po_send.at[j - 1],
            recv_sem=po_recv.at[j - 1],
            device_id=at_x(x_n - j),
            device_id_type=MESH,
        )

    pieces = column_pieces(width)

    def y_copy(side, p, j):
        cols = pl.ds(*pieces[p])
        return pltpu.make_async_remote_copy(
            src_ref=gsend.at[side, lax.rem(y_me + j, y_n), :, cols],
            dst_ref=gin.at[side, j - 1, :, cols],
            send_sem=y_send.at[side, p, j - 1],
            recv_sem=y_recv.at[side, p, j - 1],
            device_id=at_y(j),
            device_id_type=MESH,
        )

    def gradient(side, p):
        where = lax.rem(zh + 1 - side, 2)
        mine = dpre_t[pl.ds(pl.multiple_of(where * quarter, quarter), quarter)]
        start, size = pieces[p]
        for at in range(start, start + size, 256):
            cols = slice(at, min(at + 256, start + size))
            term = jnp.dot(mine, xs[:, cols], preferred_element_type=F32)
            gsend[side, :, :, cols] = term.astype(BF16).reshape(y_n, block, cols.stop - cols.start)
        for j in range(1, y_n):
            y_copy(side, p, j).start()

    def summed(side, p):
        start, size = pieces[p]
        cols = slice(start, start + size)
        for j in range(1, y_n):
            y_copy(side, p, j).wait_recv()
        total = gsend[side, pl.ds(y_me, 1), :, cols][0].astype(F32)
        for j in range(1, y_n):
            total = total + gin[side, j - 1, :, cols].astype(F32)
        return total

    def zz_copy(p):
        cols = pl.ds(*pieces[p])
        return pltpu.make_async_remote_copy(
            src_ref=zsend.at[:, cols],
            dst_ref=zin.at[:, cols],
            send_sem=zz_send.at[p],
            recv_sem=zz_recv.at[p],
            device_id=across,
            device_id_type=MESH,
        )

    def cross(p):
        start, size = pieces[p]
        zsend[:, start:start + size] = summed(0, p).astype(BF16)
        zz_copy(p).start()

    hidden(0)
    for p in range(min(2, len(pieces))):
        gradient(0, p)
    hidden(1)
    cross(0)
    for p in range(2, len(pieces)):
        gradient(0, p)
    cross(1)
    project_out()
    for p in range(2, len(pieces)):
        cross(p)

    for j in range(1, x_n):
        po_copy(j).wait_recv()
    out = own_po[...]
    for j in range(1, x_n):
        out = out + po_in[j - 1].reshape(slots, width).astype(F32)
    back_rows[...] = out.astype(BF16).reshape(experts, 2, width)

    def ret_copy(z_to, c, slot):
        return pltpu.make_async_remote_copy(
            src_ref=back_rows.at[slot + c],
            dst_ref=ret.at[e_me],
            send_sem=r_send.at[slot + c],
            recv_sem=r_recv.at[e_me],
            device_id=at_z(z_to, c),
            device_id_type=MESH,
        )

    def ret_start(m, carry):
        slot = 4 * m - 2
        for z, add in ((wrap(z_me - m), 0), (wrap(z_me + m), 2)):
            for c in (0, 1):
                ret_copy(z, c, slot + add).start()
        return carry

    lax.fori_loop(1, half, ret_start, 0)
    for c in (0, 1):
        ret_copy(wrap(z_me - half + zl_n * core), c, experts - 2).start()
    mate_back = pltpu.make_async_remote_copy(
        src_ref=back_rows.at[1 - core],
        dst_ref=ret.at[e_me],
        send_sem=r_send.at[0],
        recv_sem=r_recv.at[e_me],
        device_id=mate,
        device_id_type=MESH,
    )
    mate_back.start()
    ret[pl.ds(e_me, 1)] = back_rows[pl.ds(core, 1)]

    for p in range(len(pieces)):
        gradient(1, p)

    def z_sent(k, carry):
        pltpu.make_async_remote_copy(
            src_ref=snd.at[0], dst_ref=xg.at[0, 0], send_sem=z_send.at[k],
            recv_sem=z_recv.at[0], device_id=mate, device_id_type=MESH,
        ).wait_send()
        return carry

    lax.fori_loop(2, experts, z_sent, 0)
    mate_copy.wait_send()
    for g in range(len(groups)):
        for j in range(1, x_n):
            x_copy(g, j).wait_send()
    for j in range(1, x_n):
        po_copy(j).wait_send()

    for p, (start, size) in enumerate(pieces):
        weight_grad[:, start:start + size] = summed(1, p)
    token = lax.broadcasted_iota(jnp.int32, (slots, toks), 1).astype(F32)
    chosen = column(place[...], slots, 1) == token
    weight = jnp.where(chosen, column(gate[...], slots, 1), 0.0).T
    high = weight.astype(BF16)
    rest = weight - high.astype(F32)
    middle = rest.astype(BF16)
    low = (rest - middle.astype(F32)).astype(BF16)
    weights = jnp.concatenate([low, middle, high], axis=1)

    def ret_arrived(e, carry):
        pltpu.make_async_remote_copy(
            src_ref=back_rows.at[0], dst_ref=ret.at[e], send_sem=r_send.at[0],
            recv_sem=r_recv.at[e], device_id=mate, device_id_type=MESH,
        ).wait_recv()
        return carry

    lax.fori_loop(0, e_me, ret_arrived, 0)
    lax.fori_loop(e_me + 1, experts, ret_arrived, 0)
    came = ret[...].reshape(slots, width)
    came = jnp.concatenate([came, came, came], axis=0)
    mixed[...] = jnp.dot(weights, came, preferred_element_type=F32).astype(BF16)

    def ret_sent(k, carry):
        pltpu.make_async_remote_copy(
            src_ref=back_rows.at[0], dst_ref=ret.at[0], send_sem=r_send.at[k],
            recv_sem=r_recv.at[0], device_id=mate, device_id_type=MESH,
        ).wait_send()
        return carry

    lax.fori_loop(2, experts, ret_sent, 0)
    mate_back.wait_send()
    for p in range(len(pieces)):
        for side in range(2):
            for j in range(1, y_n):
                y_copy(side, p, j).wait_send()

    for p, (start, size) in enumerate(pieces):
        zz_copy(p).wait_recv()
        cols = slice(start, start + size)
        weight_grad[:, cols] += zin[:, cols].astype(F32)
    for p in range(len(pieces)):
        zz_copy(p).wait_send()


def body(zl_n, y_n, x_n, tokens, grad_out, slot_token, slot_gate, w_in, w_out):
    experts = 2 * zl_n
    toks, width = tokens.shape
    hid = w_in.shape[1]
    slots = 2 * experts
    rows = x_n * slots
    block = hid // (2 * y_n)
    groups = len(arrival_groups(experts))
    pieces = len(column_pieces(width))
    vmem = pl.BlockSpec(memory_space=pltpu.VMEM)
    hbm = pl.BlockSpec(memory_space=pl.ANY)
    dma = pltpu.SemaphoreType.DMA
    mixed, weight_grad = pl.pallas_call(
        functools.partial(layer_kernel, (zl_n, x_n, y_n)),
        out_shape=(
            jax.ShapeDtypeStruct((toks, width), BF16),
            jax.ShapeDtypeStruct((block, width), F32),
        ),
        in_specs=[vmem] * 4 + [hbm] * 2,
        out_specs=(vmem, vmem),
        scratch_shapes=[
            pltpu.VMEM((hid, width), BF16),
            pltpu.VMEM((hid, width), BF16),
            pltpu.VMEM((experts, 4, width), BF16),
            pltpu.VMEM((x_n, experts, 4, width), BF16),
            pltpu.VMEM((rows, width), BF16),
            pltpu.VMEM((rows, width), BF16),
            pltpu.VMEM((rows, hid), BF16),
            pltpu.VMEM((hid, rows), BF16),
            pltpu.VMEM((x_n - 1, experts, 2, width), BF16),
            pltpu.VMEM((x_n - 1, experts, 2, width), BF16),
            pltpu.VMEM((slots, width), F32),
            pltpu.VMEM((experts, 2, width), BF16),
            pltpu.VMEM((experts, 2, width), BF16),
            pltpu.VMEM((2, y_n, block, width), BF16),
            pltpu.VMEM((2, y_n - 1, block, width), BF16),
            pltpu.VMEM((block, width), BF16),
            pltpu.VMEM((block, width), BF16),
            dma((2,)),
            dma((experts,)),
            dma((experts,)),
            dma((groups, x_n)),
            dma((groups, x_n)),
            dma((x_n,)),
            dma((x_n,)),
            dma((experts,)),
            dma((experts,)),
            dma((2, pieces, y_n)),
            dma((2, pieces, y_n)),
            dma((pieces,)),
            dma((pieces,)),
        ],
        compiler_params=pltpu.CompilerParams(
            collective_id=0, has_side_effects=True, vmem_limit_bytes=56 * 1024 * 1024
        ),
    )(
        slot_token.reshape(experts, 2).T, slot_gate.reshape(experts, 2).T,
        tokens, grad_out, w_in[0], w_out[0],
    )
    return mixed, weight_grad[None]


def solution(mesh):
    placed = (
        P(("expert", "fsdp", "dp"), None),
        P(("expert", "fsdp", "dp"), None),
        P(("expert", "fsdp", "dp"), None, None),
        P(("expert", "fsdp", "dp"), None, None),
        P("expert", "fsdp", None),
        P("expert", "fsdp", None),
    )
    sizes = (mesh.shape["expert"] // 2, mesh.shape["dp"] // 2, mesh.shape["fsdp"])
    return jax.shard_map(
        functools.partial(body, *sizes),
        mesh=mesh,
        in_specs=placed,
        out_specs=(P(("expert", "fsdp", "dp"), None), P("expert", ("fsdp", "dp"), None)),
        check_vma=False,
    )
```
